256 devices in a mesh: rows: 8 (over z_lo, x), cols: 32 (over y, z_hi, core).
Axes of the slice: x: 4, y: 4, z: 8 (z_hi: 4, z_lo: 2; z = z_hi * 2 + z_lo), core: 2. Of those that a mesh axis runs over, the one named last changes fastest.
Arguments:
- image: bfloat16 [3, 512, 32768], P(None, 'rows', 'cols'), may hold values from -6 to 6
- w_patch: bfloat16 [48, 256], replicated, may hold values from -0.875 to 0.875
- dw_kernel: bfloat16 [7, 7, 256], replicated, may hold values from -0.875 to 0.875
- gain_one: float32 [256], replicated, may hold values from 0.25 to 1.75
- w_up: bfloat16 [256, 1024], replicated, may hold values from -0.375 to 0.375
- w_down: bfloat16 [1024, 256], replicated, may hold values from -0.1875 to 0.1875
- scale_block: float32 [256], replicated, may hold values from 0.25 to 1.75
- gain_two: float32 [256], replicated, may hold values from 0.25 to 1.75
- w_kv: bfloat16 [256, 2048], replicated, may hold values from -0.375 to 0.375
- latents: bfloat16 [128, 1024], replicated, may hold values from -0.75 to 0.75
- gain_three: float32 [1024], replicated, may hold values from 0.25 to 1.75
- w_q: bfloat16 [1024, 1024], replicated
- w_o: bfloat16 [1024, 1024], replicated, may hold values from -0.1875 to 0.1875
Outputs:
- encoded: float32 [128, 1024], replicated
The draws below stay inside these ranges and needn't reach their ends.
All inputs are finite; a program needn't handle non-finite values.
Results may differ from the reference program's by a relative error of at most 0.0117.
The reference program's roundings to bfloat16 on the way (of `embed`, `normed`, `hidden`, `features`, `query`, `probs` and `attended`) count: a program that leaves them out, or rounds other values in their place, can miss the bound.
Values may be sent and summed in bfloat16 or wider, within the bound.
No kernel may reach another device: no remote copies, remote signals or barrier semaphores. Data moves between devices by JAX's collectives and lax.ppermute only.
A program may use at most 320 MiB of HBM per device.

```python
import jax
import jax.numpy as jnp
from jax import lax

C = 256
HID = 1024
HEADS = 8
HEAD_DIM = 128
LAT = 128
TH = 16
DK = 1024
GH = 128
GW = 8192
N_ROWS = 8


def draw_w_q(key, part):
    base_key = jax.random.fold_in(key, 11)
    head_key = jax.random.fold_in(key, 23)
    base = jax.random.truncated_normal(base_key, -4.0, 4.0, (DK, DK), jnp.float32) * DK ** (-0.5)
    head_scale = jnp.exp(jax.random.uniform(head_key, (HEADS,), jnp.float32, jnp.log(2.0), jnp.log(32.0)))
    return (base * jnp.repeat(head_scale, HEAD_DIM)[None, :]).astype(jnp.bfloat16)


def levels(key, shape, split, low, high):
    loudness = 1.0
    for dim, blocks in split:
        draws = jax.random.uniform(jax.random.fold_in(jax.random.fold_in(key, 6), dim), (blocks,), jnp.float32, low / len(split), high / len(split))
        loudness = loudness * jnp.repeat(jnp.exp(draws), shape[dim] // blocks).reshape((-1,) + (1,) * (len(shape) - 1 - dim))
    return loudness


def gaussian(rng, extent, scale, limit, pieces=(), kind=jnp.bfloat16):
    factor_of = levels(rng, extent, pieces, -0.22, 0.18) if pieces else 1.0
    values = jax.random.normal(rng, extent, jnp.float32) * scale * factor_of
    return jnp.minimum(jnp.maximum(values, -limit), limit).astype(kind)


def setup_inputs(seed: int = 0) -> dict:
    key_list = jax.random.split(jax.random.key(seed), 14)
    return {
        "image": gaussian(key_list[0], (3, 4 * GH, 4 * GW), 1.0, 6.0, ((1, 8), (2, 32))),
        "w_patch": gaussian(key_list[1], (48, C), 48 ** -0.5, 0.875),
        "dw_kernel": gaussian(key_list[2], (7, 7, C), 49 ** -0.5, 0.875),
        "gain_one": jnp.clip(1.0 + 0.15 * jax.random.normal(key_list[3], (C,), jnp.float32), 0.25, 1.75),
        "w_up": gaussian(key_list[4], (C, HID), C ** -0.5, 0.375),
        "w_down": gaussian(key_list[5], (HID, C), HID ** -0.5, 0.1875),
        "scale_block": jnp.clip(1.0 + 0.15 * jax.random.normal(key_list[6], (C,), jnp.float32), 0.25, 1.75),
        "gain_two": jnp.clip(1.0 + 0.15 * jax.random.normal(key_list[7], (C,), jnp.float32), 0.25, 1.75),
        "w_kv": gaussian(key_list[8], (C, 2 * DK), C ** -0.5, 0.375),
        "latents": gaussian(key_list[9], (LAT, DK), 0.05, 0.75),
        "gain_three": jnp.clip(1.0 + 0.15 * jax.random.normal(key_list[10], (DK,), jnp.float32), 0.25, 1.75),
        "w_q": draw_w_q(jax.random.fold_in(key_list[13], 71), 0),
        "w_o": gaussian(key_list[12], (DK, DK), DK ** -0.5, 0.1875),
    }


def layer_norm(values, gain):
    center = values - lax.optimization_barrier(jnp.mean(values, axis=-1, keepdims=True))
    spread = lax.optimization_barrier(jnp.mean(center * center, axis=-1, keepdims=True))
    return center * lax.rsqrt(spread + 1e-06) * gain

def reference(image, w_patch, dw_kernel, gain_one, w_up, w_down, scale_block, gain_two, w_kv, latents, gain_three, w_q, w_o):
    padded_image = jnp.pad(image, ((0, 0), (12, 12), (12, 12)))
    lat_norm = layer_norm(latents.astype(jnp.float32), gain_three).astype(jnp.bfloat16)
    query = (jnp.dot(lat_norm, w_q, preferred_element_type=jnp.float32) * HEAD_DIM ** (-0.5)).astype(jnp.bfloat16)
    query_heads = query.reshape(LAT, HEADS, HEAD_DIM).astype(jnp.float32)
    kernel = dw_kernel.astype(jnp.float32)

    def block_step(carry, index):
        top_run, total_run, accum_run = carry
        strip = lax.dynamic_slice_in_dim(padded_image, index * (4 * TH), 4 * (TH + 6), 1)
        patches = strip.reshape(3, TH + 6, 4, GW + 6, 4).transpose(1, 3, 0, 2, 4).reshape((TH + 6) * (GW + 6), 48)
        embed = jnp.dot(patches, w_patch, preferred_element_type=jnp.float32).astype(jnp.bfloat16)
        embed = embed.reshape(TH + 6, GW + 6, C)
        mixed = jnp.zeros((TH, GW, C), jnp.float32)
        for offset_row in range(7):
            for offset_col in range(7):
                mixed = mixed + embed[offset_row:offset_row + TH, offset_col:offset_col + GW].astype(jnp.float32) * kernel[offset_row, offset_col]
        normed = layer_norm(mixed.reshape(TH * GW, C), gain_one).astype(jnp.bfloat16)
        hidden = jax.nn.gelu(jnp.dot(normed, w_up, preferred_element_type=jnp.float32)).astype(jnp.bfloat16)
        center = embed[3:3 + TH, 3:3 + GW].reshape(TH * GW, C).astype(jnp.float32)
        block = center + scale_block * jnp.dot(hidden, w_down, preferred_element_type=jnp.float32)
        features = layer_norm(block, gain_two).astype(jnp.bfloat16)
        keyval = jnp.dot(features, w_kv, preferred_element_type=jnp.float32).astype(jnp.bfloat16)
        keys = keyval[:, :DK].reshape(TH * GW, HEADS, HEAD_DIM).astype(jnp.float32)
        values = keyval[:, DK:].reshape(TH * GW, HEADS, HEAD_DIM).astype(jnp.float32)
        scores = jnp.einsum('lhd,thd->hlt', query_heads, keys)
        top_new = jnp.maximum(top_run, lax.optimization_barrier(jnp.max(scores, axis=-1)))
        expo = jnp.exp(scores - top_new[:, :, None])
        probs = expo.astype(jnp.bfloat16).astype(jnp.float32)
        factor = jnp.exp(top_run - top_new)
        total_new = total_run * factor + lax.optimization_barrier(jnp.sum(expo, axis=-1))
        accum_new = accum_run * factor[:, :, None] + jnp.einsum('hlt,thd->hld', probs, values)
        return ((top_new, total_new, accum_new), None)
    init = (jnp.full((HEADS, LAT), -1e+30, jnp.float32), jnp.zeros((HEADS, LAT), jnp.float32), jnp.zeros((HEADS, LAT, HEAD_DIM), jnp.float32))
    (top_run, total_run, accum_run), _ = lax.scan(block_step, init, jnp.arange(N_ROWS, dtype=jnp.int32))
    attended = (accum_run / total_run[:, :, None]).transpose(1, 0, 2).reshape(LAT, DK).astype(jnp.bfloat16)
    return latents.astype(jnp.float32) + jnp.dot(attended, w_o, preferred_element_type=jnp.float32)
```

```python
import jax
import jax.numpy as jnp
from jax import lax
from jax.sharding import PartitionSpec as P

HEADS = 8
HEAD_DIM = 128


def with_halo(value, sides, width):
    for axis, dim in sides:
        devices, length = (lax.axis_size(axis), value.shape[dim])
        up = [(i, (i + 1) % devices) for i in range(devices - 1)]
        down = [(j, i) for i, j in up]
        last = lax.slice_in_dim(value, length - width, length, axis=dim)
        initial = lax.slice_in_dim(value, 0, width, axis=dim)
        before = lax.ppermute(last, axis, up)
        after = lax.ppermute(initial, axis, down)
        value = jnp.concatenate([before, value, after], axis=dim)
    return value


def layer_norm(values, gain):
    center = values - jnp.mean(values, axis=-1, keepdims=True)
    spread = jnp.mean(center * center, axis=-1, keepdims=True)
    return center * lax.rsqrt(spread + 1e-06) * gain


def stem_patches(pixels, w_patch, grid_rows, grid_cols):
    patches = (
        pixels.reshape(3, grid_rows, 4, grid_cols, 4)
        .transpose(1, 3, 0, 2, 4)
        .reshape(grid_rows * grid_cols, 48)
    )
    embed = jnp.dot(patches, w_patch, preferred_element_type=jnp.float32).astype(jnp.bfloat16)
    return embed.reshape(grid_rows, grid_cols, w_patch.shape[1])


def split_three(value):
    high = lax.reduce_precision(value, 8, 7)
    rest = value - high
    middle = lax.reduce_precision(rest, 8, 7)
    return high, middle, rest - middle


def pack_partial(sums, top, total):
    rows = jnp.stack([*split_three(top), *split_three(total)], axis=-2)
    rows = jnp.pad(rows, ((0, 0),) * (rows.ndim - 2) + ((0, 10), (0, 0)))
    return jnp.concatenate([sums, rows], axis=-2).astype(jnp.bfloat16)


def merge_partials(packed):
    packed = packed.astype(jnp.float32)
    count = packed.shape[1] - 16
    stats = packed[:, count:]
    top = (stats[:, 0] + stats[:, 1]) + stats[:, 2]
    total = (stats[:, 3] + stats[:, 4]) + stats[:, 5]
    top_all = jnp.max(top, axis=0)
    factor = jnp.exp(top - top_all)
    sums = jnp.sum(packed[:, :count] * factor[:, None], axis=0)
    return sums, top_all, jnp.sum(total * factor, axis=0)


def share(value, axis):
    size = lax.axis_size(axis)
    return lax.all_to_all(jnp.broadcast_to(value, (size, *value.shape)), axis, 0, 0)


def body(
    image,
    w_patch,
    dw_kernel,
    gain_one,
    w_up,
    w_down,
    scale_block,
    gain_two,
    w_kv,
    latents,
    gain_three,
    w_q,
    w_o,
):
    tile_rows = image.shape[1] // 4
    tile_cols = image.shape[2] // 4
    count = tile_rows * tile_cols
    width = w_patch.shape[1]
    embed = stem_patches(image, w_patch, tile_rows, tile_cols)
    padded = with_halo(embed, (("rows", 0), ("cols", 1)), 3)
    kernel = dw_kernel.astype(jnp.float32)
    mixed = jnp.zeros((tile_rows, tile_cols, width), jnp.float32)
    for offset_row in range(7):
        for offset_col in range(7):
            mixed = (
                mixed
                + padded[
                    offset_row : offset_row + tile_rows, offset_col : offset_col + tile_cols
                ].astype(jnp.float32)
                * kernel[offset_row, offset_col]
            )
    normed = layer_norm(mixed.reshape(count, width), gain_one).astype(jnp.bfloat16)
    hidden = jax.nn.gelu(jnp.dot(normed, w_up, preferred_element_type=jnp.float32)).astype(
        jnp.bfloat16
    )
    block = embed.reshape(count, width).astype(jnp.float32) + scale_block * jnp.dot(
        hidden, w_down, preferred_element_type=jnp.float32
    )
    features = layer_norm(block, gain_two).astype(jnp.bfloat16)
    keyval = jnp.dot(features, w_kv, preferred_element_type=jnp.float32).astype(jnp.bfloat16)
    kv_width = HEADS * HEAD_DIM
    keys = keyval[:, :kv_width].reshape(count, HEADS, HEAD_DIM)
    values = keyval[:, kv_width:].reshape(count, HEADS, HEAD_DIM)
    lat_norm = layer_norm(latents.astype(jnp.float32), gain_three).astype(jnp.bfloat16)
    query = (
        jnp.dot(lat_norm, w_q, preferred_element_type=jnp.float32) * HEAD_DIM ** (-0.5)
    ).astype(jnp.bfloat16)
    query_heads = query.reshape(latents.shape[0], HEADS, HEAD_DIM)
    scores = jnp.einsum("lhd,thd->hlt", query_heads, keys, preferred_element_type=jnp.float32)
    top_local = jnp.max(scores, axis=-1)
    expo = jnp.exp(scores - top_local[:, :, None])
    total_local = jnp.sum(expo, axis=-1)
    accum_local = jnp.einsum(
        "hlt,thd->hld", expo.astype(jnp.bfloat16), values, preferred_element_type=jnp.float32
    )
    cols = lax.axis_size("cols")
    per_head = cols // HEADS
    sums = accum_local.transpose(0, 2, 1).reshape(cols, kv_width // cols, -1)
    packed = pack_partial(
        sums, jnp.repeat(top_local, per_head, axis=0), jnp.repeat(total_local, per_head, axis=0)
    )
    partial = merge_partials(lax.all_to_all(packed, "cols", 0, 0))
    sums, _, total = merge_partials(share(pack_partial(*partial), "rows"))
    attended = share((sums / total).astype(jnp.bfloat16), "cols").reshape(kv_width, -1)
    return latents.astype(jnp.float32) + lax.dot_general(
        attended, w_o, (((0,), (0,)), ((), ())), preferred_element_type=jnp.float32
    )


def solution(mesh):
    in_specs = (P(None, "rows", "cols"), P(), P(), P(), P(), P(), P(), P(), P(), P(), P(), P(), P())
    out_specs = P()
    return jax.shard_map(body, mesh=mesh, in_specs=in_specs, out_specs=out_specs, check_vma=False)
```

```python
import jax
import jax.numpy as jnp
from jax import lax
from jax.experimental import pallas as pl
from jax.experimental.pallas import tpu as pltpu
from jax.sharding import PartitionSpec as P

HEADS = 8
HEAD_DIM = 128
F32 = jnp.float32
BF16 = jnp.bfloat16
TOKENS = 512


def exchange(value, axis, dim, width):
    devices, length = lax.axis_size(axis), value.shape[dim]
    up = [(i, i + 1) for i in range(devices - 1)]
    down = [(j, i) for i, j in up]
    before = lax.ppermute(lax.slice_in_dim(value, length - width, length, axis=dim), axis, up)
    after = lax.ppermute(lax.slice_in_dim(value, 0, width, axis=dim), axis, down)
    return before, after


def layer_norm(values, gain):
    center = values - jnp.mean(values, axis=-1, keepdims=True)
    spread = jnp.mean(center * center, axis=-1, keepdims=True)
    return center * lax.rsqrt(spread + 1e-06) * gain


def matmul(left, right, dims=((1,), (0,))):
    return lax.dot_general(left, right, (dims, ((), ())), preferred_element_type=F32)


def iota(shape, dim):
    return lax.broadcasted_iota(jnp.int32, shape, dim)


def ones_where(mask):
    return jnp.where(mask, 1.0, 0.0).astype(BF16)


def stem(image, side, edge, w_patch, embed, ordered, pixels):
    rows = embed.shape[0]
    local = (rows - 6) * 4
    places = rows * 16
    place, source = iota((places, 3 * local), 0), iota((places, 3 * local), 1)
    slot = place % 16
    pixel_row = (place // 16) * 4 + slot % 4
    channel = slot // 4
    inside = (slot < 12) & (pixel_row >= 12) & (pixel_row < 12 + local)
    pick = ones_where(inside & (source == channel * local + pixel_row - 12))
    place, source = iota((places, 96), 0), iota((places, 96), 1)
    slot = place % 16
    pixel_row = (place // 16) * 4 + slot % 4
    channel = slot // 4
    upper = (pixel_row < 12) & (source == channel * 16 + pixel_row)
    lower = (pixel_row >= 12 + local) & (source == 48 + channel * 16 + pixel_row - 12 - local)
    pick_edge = ones_where((slot < 12) & (upper | lower))
    width = image.shape[1]
    for start in range(0, width, 256):
        lanes = slice(start, start + 256)
        ordered[:, lanes] = (
            matmul(pick, image[:, lanes]) + matmul(pick_edge, edge[:, lanes])
        ).astype(BF16)
    ordered[:, width:] = (
        matmul(pick, side[...]) + matmul(pick_edge, edge[:, width:])
    ).astype(BF16)
    lane, pixel = iota((512, 512), 1), iota((512, 512), 0)
    split = ones_where(pixel == 4 * (lane % 128) + lane // 128)
    for part in range(width // 512):
        found = matmul(ordered[:, part * 512 : part * 512 + 512], split).astype(BF16)
        for phase in range(4):
            pixels[phase, :, part * 128 : part * 128 + 128] = found[:, phase * 128 : phase * 128 + 128]
    lane, pixel = iota((128, 512), 1), iota((128, 512), 0)
    split = ones_where((pixel < 24) & (pixel == 4 * (lane % 128 - 5) + lane // 128))
    found = matmul(ordered[:, width:], split).astype(BF16)
    columns = width // 4
    for phase in range(4):
        pixels[phase, :, columns:] = found[:, phase * 128 : phase * 128 + 128]
    place, source = iota((64, 48), 0), iota((64, 48), 1)
    slot = place % 16
    pick = ones_where((slot < 12) & (source == slot * 4 + place // 16))
    weights = matmul(pick, w_patch[...]).astype(BF16)

    def step(row, carry):
        patches = jnp.concatenate(
            [pixels[phase, pl.ds(pl.multiple_of(row * 16, 16), 16), :] for phase in range(4)], axis=0
        )
        value = matmul(patches, weights, ((0,), (0,))).astype(BF16).astype(F32)
        blocks = columns // 8
        embed[row, 1 : blocks + 1] = value[:columns].reshape(blocks, 8, -1)
        embed[row, 0] = value[columns : columns + 8]
        embed[row, blocks + 1] = value[columns + 8 : columns + 16]
        return carry

    lax.fori_loop(0, rows, step, 0)


def conv_tile(embed, taps, mixed_ref, row, store_row, rows=2, blocks=8):
    columns = embed.shape[1] - 2
    row_in_lane = iota((1, 8, 128), 1)
    chunks = columns // blocks

    def step(index, carry):
        block = (index % chunks) * blocks
        half = index // chunks
        lanes = pl.ds(pl.multiple_of(half * 128, 128), 128)
        mixed = [None] * rows
        for shift in range(7):
            first, rest = divmod(5 + shift, 8)
            count = blocks + (1 if rest else 0)
            sums = [None] * rows
            weights = [taps[i * 7 + shift, :, lanes] for i in range(7)]
            for line in range(rows + 6):
                value = embed[row + line, pl.ds(block + first, count), :, lanes]
                for r in range(rows):
                    if 0 <= line - r < 7:
                        term = value * weights[line - r]
                        sums[r] = term if sums[r] is None else sums[r] + term
            for r in range(rows):
                total = sums[r]
                if rest:
                    turned = pltpu.roll(total, 8 - rest, 1)
                    total = jnp.where(row_in_lane < 8 - rest, turned[:blocks], turned[1:])
                mixed[r] = total if mixed[r] is None else mixed[r] + total
        for r in range(rows):
            mixed_ref[store_row + r, pl.ds(block, blocks), :, lanes] = mixed[r]
        return carry

    lax.fori_loop(0, 2 * chunks, step, 0)


def gelu_half(half):
    c = 2.0 * 0.7978845608028654
    inner = half * (c + (c * 4.0 * 0.044715) * (half * half))
    return half + half * jnp.tanh(inner)


def encoder(
    image, side, edge, w_patch, taps, gain_one, w_up, w_down, scale, gain_two, w_keys, w_values, query,
    out, embed, ordered, pixels, mixed, features, sums,
):
    rows = embed.shape[0] - 6
    columns = (embed.shape[1] - 2) * 8
    width = embed.shape[3]
    stem(image, side, edge, w_patch, embed, ordered, pixels)
    per_tile = TOKENS // columns
    tiles = rows // per_tile

    def block_step(tile, carry):
        row = tile * per_tile
        conv_tile(embed, taps, mixed, row, 0)
        normed = layer_norm(mixed[...].reshape(TOKENS, width), gain_one[...]).astype(BF16)
        down = None
        for start in range(0, w_up.shape[1], 256):
            hidden = gelu_half(matmul(normed, w_up[:, start : start + 256])).astype(BF16)
            part = matmul(hidden, w_down[start : start + 256, :])
            down = part if down is None else down + part
        center = embed[pl.ds(row + 3, per_tile), 1 : columns // 8 + 1].reshape(TOKENS, width)
        block = center + scale[...] * down
        features[pl.ds(pl.multiple_of(tile * TOKENS, TOKENS), TOKENS), :] = layer_norm(
            block, gain_two[...]
        ).astype(BF16)
        return carry

    lax.fori_loop(0, tiles, block_step, 0)
    pair = 2 * HEAD_DIM
    sums[...] = jnp.zeros_like(sums)
    latents = out.shape[2]
    lowest = jnp.full((1, 2 * latents), -jnp.inf, F32)
    start_stats = tuple((lowest, jnp.zeros((1, 2 * latents), F32)) for _ in range(HEADS // 2))

    def attend_step(tile, stats):
        feature = features[pl.ds(pl.multiple_of(tile * TOKENS, TOKENS), TOKENS), :]
        turned = feature.T
        result = []
        for p in range(HEADS // 2):
            top, total = stats[p]
            keys = matmul(feature, w_keys[:, p * pair : p * pair + pair]).astype(BF16)
            scores = matmul(keys, query[p])
            top_new = jnp.maximum(top, jnp.max(scores, axis=0, keepdims=True))
            expo = jnp.exp(scores - top_new)
            factor = jnp.exp(top - top_new)
            total = total * factor + jnp.sum(expo, axis=0, keepdims=True)
            lanes = slice(p * 2 * latents, (p + 1) * 2 * latents)
            sums[:, lanes] = sums[:, lanes] * factor + matmul(turned, expo.astype(BF16))
            result.append((top_new, total))
        return tuple(result)

    stats = lax.fori_loop(0, tiles, attend_step, start_stats)
    per_head = out.shape[0] // HEADS
    depth = HEAD_DIM // per_head
    for head in range(HEADS):
        lanes = slice(head * latents, (head + 1) * latents)
        mine = slice((head % 2) * latents, (head % 2 + 1) * latents)
        total_sums = sums[:, lanes]
        high = total_sums.astype(BF16)
        low = (total_sums - high.astype(F32)).astype(BF16)
        weights = w_values[:, head * HEAD_DIM : (head + 1) * HEAD_DIM]
        value = matmul(weights, high, ((0,), (0,))) + matmul(weights, low, ((0,), (0,)))
        lines = []
        for stat in stats[head // 2]:
            rest = stat[:, mine]
            for _ in range(3):
                piece = rest.astype(BF16).astype(F32)
                lines.append(piece)
                rest = rest - piece
        line = iota((16, latents), 0)
        extra = jnp.zeros((16, latents), F32)
        for k, piece in enumerate(lines):
            extra = jnp.where(line == k, piece, extra)
        for part in range(per_head):
            place = head * per_head + part
            out[place, :depth] = value[part * depth : (part + 1) * depth].astype(BF16)
            out[place, depth:] = extra.astype(BF16)


def split_three(value):
    high = lax.reduce_precision(value, 8, 7)
    rest = value - high
    middle = lax.reduce_precision(rest, 8, 7)
    return high, middle, rest - middle


def pack_partial(sums, top, total):
    rows = jnp.stack([*split_three(top), *split_three(total)], axis=-2)
    rows = jnp.pad(rows, ((0, 0),) * (rows.ndim - 2) + ((0, 10), (0, 0)))
    return jnp.concatenate([sums, rows], axis=-2).astype(BF16)


def merge_partials(packed):
    packed = packed.astype(F32)
    count = packed.shape[1] - 16
    stats = packed[:, count:]
    top = (stats[:, 0] + stats[:, 1]) + stats[:, 2]
    total = (stats[:, 3] + stats[:, 4]) + stats[:, 5]
    top_all = jnp.max(top, axis=0)
    factor = jnp.exp(top - top_all)
    sums = jnp.sum(packed[:, :count] * factor[:, None], axis=0)
    return sums, top_all, jnp.sum(total * factor, axis=0)


def share(value, axis):
    size = lax.axis_size(axis)
    return lax.all_to_all(jnp.broadcast_to(value, (size, *value.shape)), axis, 0, 0)


def partial_sums(
    image, side, edge, w_patch, dw_kernel, gain_one, w_up, w_down, scale_block, gain_two, w_kv, pairs, cols
):
    channels, height, breadth = image.shape
    tile_rows, tile_cols = height // 4, breadth // 4
    count, width = pairs.shape[2] // 2, w_patch.shape[1]
    kv_width = HEADS * HEAD_DIM
    taps = jnp.broadcast_to(dw_kernel.astype(F32).reshape(49, 1, width), (49, 8, width))
    return pl.pallas_call(
        encoder,
        out_shape=jax.ShapeDtypeStruct((cols, kv_width // cols + 16, count), BF16),
        in_specs=[pl.BlockSpec(memory_space=pltpu.VMEM)] * 13,
        out_specs=pl.BlockSpec(memory_space=pltpu.VMEM),
        scratch_shapes=[
            pltpu.VMEM((tile_rows + 6, tile_cols // 8 + 2, 8, width), F32),
            pltpu.VMEM(((tile_rows + 6) * 16, breadth + 128), BF16),
            pltpu.VMEM((4, (tile_rows + 6) * 16, tile_cols + 128), BF16),
            pltpu.VMEM((TOKENS // tile_cols, tile_cols // 8, 8, width), F32),
            pltpu.VMEM((tile_rows * tile_cols, width), BF16),
            pltpu.VMEM((width, HEADS * count), F32),
        ],
        compiler_params=pltpu.CompilerParams(vmem_limit_bytes=48 * 2**20),
        name="encoder",
    )(
        image.reshape(channels * height, breadth),
        side.reshape(channels * height, 128),
        edge.reshape(96, breadth + 128),
        w_patch,
        taps,
        gain_one.reshape(1, width),
        w_up * jnp.asarray(0.5, BF16),
        w_down,
        scale_block.reshape(1, width),
        gain_two.reshape(1, width),
        w_kv[:, :kv_width],
        w_kv[:, kv_width:],
        pairs,
    )


def body(
    image,
    w_patch,
    dw_kernel,
    gain_one,
    w_up,
    w_down,
    scale_block,
    gain_two,
    w_kv,
    latents,
    gain_three,
    w_q,
    w_o,
):
    channels, height = image.shape[:2]
    count = latents.shape[0]
    kv_width = HEADS * HEAD_DIM
    cols = lax.axis_size("cols")
    left, right = exchange(image, "cols", 2, 12)
    side = jnp.concatenate(
        [left, right, jnp.zeros((channels, height, 104), image.dtype)], axis=2
    )
    wide = jnp.concatenate([image, side], axis=2)
    above, below = exchange(wide, "rows", 1, 12)
    edge = jnp.pad(jnp.concatenate([above, below], axis=0), ((0, 0), (0, 4), (0, 0)))
    lat_norm = layer_norm(latents.astype(F32), gain_three).astype(BF16)
    query = (jnp.dot(lat_norm, w_q, preferred_element_type=F32) * HEAD_DIM ** (-0.5)).astype(BF16)
    heads = query.reshape(count, HEADS // 2, 2, HEAD_DIM).transpose(1, 2, 3, 0)
    pairs = jnp.einsum("pidl,ij->pidjl", heads, jnp.eye(2, dtype=BF16)).reshape(
        HEADS // 2, 2 * HEAD_DIM, 2 * count
    )
    packed = partial_sums(
        image, side, edge, w_patch, dw_kernel, gain_one, w_up, w_down, scale_block, gain_two, w_kv, pairs, cols
    )
    partial = merge_partials(lax.all_to_all(packed, "cols", 0, 0))
    sums, _, total = merge_partials(share(pack_partial(*partial), "rows"))
    attended = share((sums / total).astype(BF16), "cols").reshape(kv_width, -1)
    return latents.astype(F32) + matmul(attended, w_o, ((0,), (0,)))


def solution(mesh):
    in_specs = (P(None, "rows", "cols"), P(), P(), P(), P(), P(), P(), P(), P(), P(), P(), P(), P())
    out_specs = P()
    return jax.shard_map(body, mesh=mesh, in_specs=in_specs, out_specs=out_specs, check_vma=False)
```

```python
import jax
import jax.numpy as jnp
from jax import lax
from jax.experimental import pallas as pl
from jax.experimental.pallas import tpu as pltpu
from jax.sharding import PartitionSpec as P

HEADS = 8
HEAD_DIM = 128
F32 = jnp.float32
BF16 = jnp.bfloat16
TOKENS = 1024
ATTEND = 1024
CONV_ROWS = 4
CONV_BLOCKS = 1
STEM = 11


def exchange(last, first, axis):
    devices = lax.axis_size(axis)
    up = [(i, i + 1) for i in range(devices - 1)]
    down = [(j, i) for i, j in up]
    return lax.ppermute(last, axis, up), lax.ppermute(first, axis, down)


def layer_norm(values, gain):
    center = values - jnp.mean(values, axis=-1, keepdims=True)
    spread = jnp.mean(center * center, axis=-1, keepdims=True)
    return center * lax.rsqrt(spread + 1e-06) * gain


def matmul(left, right, dims=((1,), (0,))):
    return lax.dot_general(left, right, (dims, ((), ())), preferred_element_type=F32)


def iota(shape, dim):
    return lax.broadcasted_iota(jnp.int32, shape, dim)


def ones_where(mask):
    return jnp.where(mask, 1.0, 0.0).astype(BF16)


SPREAD = (
    (1, 0, -5.25, 0, 5.25, 0, -1, 0),
    (0, 1, 1, -4.25, -4.25, 1, 1, 0),
    (0, -1, 1, 4.25, -4.25, -1, 1, 0),
    (0, 0.5, 0.25, -2.5, -1.25, 2, 1, 0),
    (0, -0.5, 0.25, 2.5, -1.25, -2, 1, 0),
    (0, 2, 4, -2.5, -5, 0.5, 1, 0),
    (0, -2, 4, 2.5, -5, -0.5, 1, 0),
    (0, -1, 0, 5.25, 0, -5.25, 0, 1),
)
POINTS = (0, 1, -1, 2, -2, 0.5, -0.5)
SCALE = (1, -2 / 9, -2 / 9, 1 / 90, 1 / 90, 32 / 45, 32 / 45, 1)


def stem(image, left, right, above, below, w_patch, dw_kernel, spread, taps, ordered, pixels, split):
    rows = spread.shape[0]
    local = (rows - 6) * 4
    places = rows * 16

    def pick_rows(count, first, wanted_of):
        place, source = iota((places, count), 0), iota((places, count), 1)
        slot = place % 16
        pixel_row = (place // 16) * 4 + slot % 4 - first
        return ones_where((slot < 12) & wanted_of(source, slot // 4, pixel_row))

    pick = pick_rows(
        3 * local, 12, lambda s, c, r: (r >= 0) & (r < local) & (s == c * local + r)
    )
    pick_above = pick_rows(48, -4, lambda s, c, r: (r < 16) & (s == c * 16 + r))
    pick_below = pick_rows(48, 12 + local, lambda s, c, r: (r >= 0) & (s == c * 16 + r))
    width = image.shape[1]
    for source, base in ((image, 0), (left, width), (right, width + 128)):
        step = min(256, source.shape[1])
        for start in range(0, source.shape[1], step):
            lanes = slice(base + start, base + start + step)
            ordered[:, lanes] = (
                matmul(pick, source[:, start : start + step])
                + matmul(pick_above, above[:, lanes])
                + matmul(pick_below, below[:, lanes])
            ).astype(BF16)
    for tile in range(pixels.shape[2] // 128):
        low = max(0, 512 * tile - 32) // 128 * 128
        high = min(width, 512 * tile + 512)
        parts = [(low, high, low)]
        if 512 * tile < 32:
            parts.append((width, width + 128, -128))
        if 512 * tile + 480 > width:
            parts.append((width + 128, width + 256, width))
        found = None
        for begin, end, first in parts:
            lane, source = iota((end - begin, 512), 1), iota((end - begin, 512), 0)
            wanted = 4 * (tile * 128 + lane % 128 - 8) + lane // 128
            part = matmul(ordered[:, begin:end], ones_where(source + first == wanted))
            found = part if found is None else found + part
        found = found.astype(BF16)
        for phase in range(4):
            pixels[phase, :, tile * 128 : tile * 128 + 128] = found[:, phase * 128 : phase * 128 + 128]
    place, source = iota((64, 48), 0), iota((64, 48), 1)
    slot = place % 16
    pick = ones_where((slot < 12) & (source == slot * 4 + place // 16))
    weights = matmul(pick, w_patch[...]).astype(BF16)
    offset = iota((64, 144), 1) - 5 - 2 * iota((64, 144), 0)
    for point in range(8):
        value = jnp.zeros((64, 144), F32)
        for m in range(8):
            if SPREAD[point][m]:
                value = jnp.where(offset == m, float(SPREAD[point][m]), value)
        split[point * 64 : point * 64 + 64] = value.astype(BF16)
    for parity in range(2):
        split[512 + parity * 64 : 576 + parity * 64] = ones_where(offset == 3 + parity)
    place, source = iota((16, 7), 0), iota((16, 7), 1)
    powers = jnp.zeros((16, 7), F32)
    for point in range(8):
        for j in range(7):
            weight = float(POINTS[point] ** j) if point < 7 else float(j == 6)
            if weight:
                powers = jnp.where((place == point) & (source == j), weight, powers)
    for i in range(7):
        value = matmul(powers.astype(BF16), dw_kernel[i])
        for point in range(8):
            taps[point, i] = jnp.broadcast_to(value[point : point + 1] * SCALE[point], taps.shape[2:])

    def step(row, carry):
        patches = jnp.concatenate(
            [pixels[phase, pl.ds(pl.multiple_of(row * 16, 16), 16), :] for phase in range(4)], axis=0
        )
        value = matmul(patches, weights, ((0,), (0,))).astype(BF16)
        for half in range(2):
            found = matmul(split[...], value[half * 128 : half * 128 + 144])
            spread[row, half] = found.reshape(spread.shape[2:])
        return carry

    lax.fori_loop(0, rows, step, 0, unroll=STEM)


def conv_tile(spread, taps, mixed, row, rows, blocks):
    chunks = 8 // blocks

    def step(index, carry):
        half = index // chunks
        block = pl.ds((index % chunks) * blocks, blocks)
        for start in range(0, spread.shape[5], 128):
            lanes = slice(start, start + 128)

            def products(point):
                sums = [None] * rows
                weights = [taps[point, i, :, lanes] for i in range(7)]
                for line in range(rows + 6):
                    value = spread[row + line, half, point, block, :, lanes]
                    for r in range(rows):
                        if 0 <= line - r < 7:
                            term = value * weights[line - r]
                            sums[r] = term if sums[r] is None else sums[r] + term
                return sums

            even, odd = products(0), products(7)
            for point, factor in ((1, 1.0), (3, 2.0), (5, 0.5)):
                plus, minus = products(point), products(point + 1)
                for r in range(rows):
                    even[r] = even[r] + (plus[r] + minus[r])
                    gap = plus[r] - minus[r]
                    odd[r] = odd[r] + (gap if factor == 1.0 else gap * factor)
            for r in range(rows):
                mixed[r, half, 0, block, :, lanes] = even[r]
                mixed[r, half, 1, block, :, lanes] = odd[r]
        return carry

    lax.fori_loop(0, 2 * chunks, step, 0)


def gelu_half(half):
    c = 2.0 * 0.7978845608028654
    inner = half * (c + (c * 4.0 * 0.044715) * (half * half))
    return half + half * jnp.tanh(inner)


def encoder(
    image, left, right, above, below, w_patch, dw_kernel, gain_one, scale, gain_two, query,
    w_up_far, w_down_far, w_kv_far,
    out, spread, taps, ordered, pixels, split, mixed, features, sums, w_up, w_down, w_kv, arrived,
):
    width = spread.shape[5]
    tokens = features.shape[0]
    copies = [
        pltpu.make_async_copy(far, near, arrived.at[k])
        for k, (far, near) in enumerate(((w_up_far, w_up), (w_down_far, w_down), (w_kv_far, w_kv)))
    ]
    for copy in copies:
        copy.start()
    stem(
        image, left, right, above, below, w_patch, dw_kernel, spread, taps, ordered, pixels, split
    )
    for copy in copies:
        copy.wait()
    w_up[...] = w_up[...] * jnp.asarray(0.5, BF16)
    per_tile = mixed.shape[0]
    tiles = tokens // TOKENS

    def block_step(tile, carry):
        row = tile * per_tile
        conv_tile(spread, taps, mixed, row, CONV_ROWS, CONV_BLOCKS)
        normed = layer_norm(mixed[...].reshape(TOKENS, width), gain_one[...]).astype(BF16)
        down = None
        for start in range(0, w_up.shape[1], 256):
            hidden = gelu_half(matmul(normed, w_up[:, start : start + 256])).astype(BF16)
            part = matmul(hidden, w_down[start : start + 256, :])
            down = part if down is None else down + part
        center = spread[pl.ds(row + 3, per_tile), :, 8:10].reshape(TOKENS, width)
        block = center + scale[...] * down
        features[pl.ds(pl.multiple_of(tile * TOKENS, TOKENS), TOKENS), :] = layer_norm(
            block, gain_two[...]
        ).astype(BF16)
        return carry

    lax.fori_loop(0, tiles, block_step, 0)
    pair = 2 * HEAD_DIM
    sums[...] = jnp.zeros_like(sums)
    latents = out.shape[2]
    lowest = jnp.full((1, 2 * latents), -jnp.inf, F32)
    start_stats = tuple((lowest, jnp.zeros((1, 2 * latents), F32)) for _ in range(HEADS // 2))

    def attend_step(tile, stats):
        feature = features[pl.ds(pl.multiple_of(tile * ATTEND, ATTEND), ATTEND), :]
        turned = feature.T
        result = []

        def score(p):
            keys = matmul(feature, w_kv[:, p * pair : p * pair + pair]).astype(BF16)
            return matmul(keys, query[p])

        ahead = score(0)
        for p in range(HEADS // 2):
            top, total = stats[p]
            scores = ahead
            if p + 1 < HEADS // 2:
                ahead = score(p + 1)
            top_new = jnp.maximum(top, jnp.max(scores, axis=0, keepdims=True))
            expo = jnp.exp(scores - top_new)
            factor = jnp.exp(top - top_new)
            total = total * factor + jnp.sum(expo, axis=0, keepdims=True)
            lanes = slice(p * 2 * latents, (p + 1) * 2 * latents)
            sums[:, lanes] = sums[:, lanes] * factor + matmul(turned, expo.astype(BF16))
            result.append((top_new, total))
        return tuple(result)

    stats = lax.fori_loop(0, tokens // ATTEND, attend_step, start_stats)
    per_head = out.shape[0] // HEADS
    depth = HEAD_DIM // per_head
    for head in range(HEADS):
        lanes = slice(head * latents, (head + 1) * latents)
        mine = slice((head % 2) * latents, (head % 2 + 1) * latents)
        total_sums = sums[:, lanes]
        high = total_sums.astype(BF16)
        low = (total_sums - high.astype(F32)).astype(BF16)
        first = HEADS * HEAD_DIM + head * HEAD_DIM
        weights = w_kv[:, first : first + HEAD_DIM]
        value = matmul(weights, high, ((0,), (0,))) + matmul(weights, low, ((0,), (0,)))
        lines = []
        for stat in stats[head // 2]:
            rest = stat[:, mine]
            for _ in range(3):
                piece = rest.astype(BF16).astype(F32)
                lines.append(piece)
                rest = rest - piece
        line = iota((16, latents), 0)
        extra = jnp.zeros((16, latents), F32)
        for k, piece in enumerate(lines):
            extra = jnp.where(line == k, piece, extra)
        for part in range(per_head):
            place = head * per_head + part
            out[place, :depth] = value[part * depth : (part + 1) * depth].astype(BF16)
            out[place, depth:] = extra.astype(BF16)


def split_three(value):
    high = lax.reduce_precision(value, 8, 7)
    rest = value - high
    middle = lax.reduce_precision(rest, 8, 7)
    return high, middle, rest - middle


def pack_partial(sums, top, total):
    rows = jnp.stack([*split_three(top), *split_three(total)], axis=-2)
    rows = jnp.pad(rows, ((0, 0),) * (rows.ndim - 2) + ((0, 10), (0, 0)))
    return jnp.concatenate([sums, rows], axis=-2).astype(BF16)


def merge_partials(packed):
    packed = packed.astype(F32)
    count = packed.shape[1] - 16
    stats = packed[:, count:]
    top = (stats[:, 0] + stats[:, 1]) + stats[:, 2]
    total = (stats[:, 3] + stats[:, 4]) + stats[:, 5]
    top_all = jnp.max(top, axis=0)
    factor = jnp.exp(top - top_all)
    sums = jnp.sum(packed[:, :count] * factor[:, None], axis=0)
    return sums, top_all, jnp.sum(total * factor, axis=0)


def share(value, axis):
    size = lax.axis_size(axis)
    return lax.all_to_all(jnp.broadcast_to(value, (size, *value.shape)), axis, 0, 0)


def queries(latents, gain, w_q, out):
    count = latents.shape[0]
    normed = layer_norm(latents[...].astype(F32), gain[...]).astype(BF16)
    for head in range(HEADS):
        lanes = slice(head * HEAD_DIM, (head + 1) * HEAD_DIM)
        query = (matmul(normed, w_q[:, lanes]) * HEAD_DIM ** (-0.5)).astype(BF16)
        turned = query.astype(F32).T.astype(BF16)
        empty = jnp.zeros((HEAD_DIM, count), BF16)
        rows = slice((head % 2) * HEAD_DIM, (head % 2 + 1) * HEAD_DIM)
        out[head // 2, rows, :count] = turned if head % 2 == 0 else empty
        out[head // 2, rows, count:] = empty if head % 2 == 0 else turned


def paired_queries(latents, gain_three, w_q):
    count, width = latents.shape
    return pl.pallas_call(
        queries,
        out_shape=jax.ShapeDtypeStruct((HEADS // 2, 2 * HEAD_DIM, 2 * count), BF16),
        in_specs=[pl.BlockSpec(memory_space=pltpu.VMEM)] * 3,
        out_specs=pl.BlockSpec(memory_space=pltpu.VMEM),
        cost_estimate=pl.CostEstimate(
            flops=2 * count * width * w_q.shape[1], bytes_accessed=2 * w_q.size, transcendentals=0
        ),
        name="queries",
    )(latents, gain_three.reshape(1, width), w_q)


def partial_sums(
    image, left, right, above, below, w_patch, dw_kernel, gain_one, w_up, w_down, scale_block, gain_two,
    w_kv, pairs, cols,
):
    channels, height, breadth = image.shape
    tile_rows, tile_cols = height // 4, breadth // 4
    count, width = pairs.shape[2] // 2, w_patch.shape[1]
    return pl.pallas_call(
        encoder,
        out_shape=jax.ShapeDtypeStruct((cols, HEADS * HEAD_DIM // cols + 16, count), BF16),
        in_specs=[pl.BlockSpec(memory_space=pltpu.VMEM)] * 11 + [pl.BlockSpec(memory_space=pl.ANY)] * 3,
        out_specs=pl.BlockSpec(memory_space=pltpu.VMEM),
        scratch_shapes=[
            pltpu.VMEM((tile_rows + 6, 2, 10, 8, 8, width), F32),
            pltpu.VMEM((8, 7, 8, width), F32),
            pltpu.VMEM(((tile_rows + 6) * 16, breadth + 256), BF16),
            pltpu.VMEM((4, (tile_rows + 6) * 16, tile_cols + 128), BF16),
            pltpu.VMEM((640, 144), BF16),
            pltpu.VMEM((TOKENS // tile_cols, 2, 2, 8, 8, width), F32),
            pltpu.VMEM((tile_rows * tile_cols, width), BF16),
            pltpu.VMEM((width, HEADS * count), F32),
            pltpu.VMEM(w_up.shape, BF16),
            pltpu.VMEM(w_down.shape, BF16),
            pltpu.VMEM(w_kv.shape, BF16),
            pltpu.SemaphoreType.DMA((3,)),
        ],
        compiler_params=pltpu.CompilerParams(vmem_limit_bytes=52 * 2**20),
        name="encoder",
    )(
        image.reshape(channels * height, breadth),
        left.reshape(channels * height, 128),
        right.reshape(channels * height, 128),
        above.reshape(channels * 16, breadth + 256),
        below.reshape(channels * 16, breadth + 256),
        w_patch,
        dw_kernel,
        gain_one.reshape(1, width),
        scale_block.reshape(1, width),
        gain_two.reshape(1, width),
        pairs,
        w_up,
        w_down,
        w_kv,
    )


def project(attended, w_o, latents, out):
    out[...] = latents[...].astype(F32) + matmul(attended[...], w_o[...], ((0,), (0,)))


def body(
    image,
    w_patch,
    dw_kernel,
    gain_one,
    w_up,
    w_down,
    scale_block,
    gain_two,
    w_kv,
    latents,
    gain_three,
    w_q,
    w_o,
):
    cols = lax.axis_size("cols")
    left, right = exchange(image[:, :, -128:], image[:, :, :128], "cols")
    above, below = exchange(
        *(
            jnp.concatenate([image[:, rows], left[:, rows], right[:, rows]], axis=2)
            for rows in (slice(-16, None), slice(0, 16))
        ),
        "rows",
    )
    pairs = paired_queries(latents, gain_three, w_q)
    packed = partial_sums(
        image, left, right, above, below, w_patch, dw_kernel, gain_one, w_up, w_down, scale_block,
        gain_two, w_kv, pairs, cols,
    )
    partial = merge_partials(lax.all_to_all(packed, "cols", 0, 0))
    sums, _, total = merge_partials(share(pack_partial(*partial), "rows"))
    attended = share((sums / total).astype(BF16), "cols").reshape(HEADS * HEAD_DIM, -1)
    return pl.pallas_call(
        project,
        out_shape=jax.ShapeDtypeStruct(latents.shape, F32),
        in_specs=[pl.BlockSpec(memory_space=pltpu.VMEM)] * 3,
        out_specs=pl.BlockSpec(memory_space=pltpu.VMEM),
        name="project",
    )(attended, w_o, latents)


def solution(mesh):
    in_specs = (P(None, "rows", "cols"), P(), P(), P(), P(), P(), P(), P(), P(), P(), P(), P(), P())
    out_specs = P()
    return jax.shard_map(body, mesh=mesh, in_specs=in_specs, out_specs=out_specs, check_vma=False)
```

```python
import jax
import jax.numpy as jnp
from jax import lax
from jax.experimental import pallas as pl
from jax.experimental.pallas import tpu as pltpu
from jax.sharding import PartitionSpec as P

HEADS = 8
HEAD_DIM = 128
F32 = jnp.float32
BF16 = jnp.bfloat16
TOKENS = 1024
ATTEND = 1024
CONV_ROWS = 4
CONV_BLOCKS = 1
STEM = 22


def exchange(last, first, axis):
    devices = lax.axis_size(axis)
    up = [(i, i + 1) for i in range(devices - 1)]
    down = [(j, i) for i, j in up]
    return lax.ppermute(last, axis, up), lax.ppermute(first, axis, down)


def layer_norm(values, gain):
    center = values - jnp.mean(values, axis=-1, keepdims=True)
    spread = jnp.mean(center * center, axis=-1, keepdims=True)
    return center * lax.rsqrt(spread + 1e-06) * gain


def matmul(left, right, dims=((1,), (0,))):
    return lax.dot_general(left, right, (dims, ((), ())), preferred_element_type=F32)


def iota(shape, dim):
    return lax.broadcasted_iota(jnp.int32, shape, dim)


def ones_where(mask):
    return jnp.where(mask, 1.0, 0.0).astype(BF16)


SPREAD = (
    (9, 0, -48.25, 0, 52.5, 0, -14.25, 0, 1, 0),
    (0, -9, -9, 39.25, 39.25, -13.25, -13.25, 1, 1, 0),
    (0, 9, -9, -39.25, 39.25, 13.25, -13.25, -1, 1, 0),
    (0, -4.5, -2.25, 23, 11.5, -20.5, -10.25, 2, 1, 0),
    (0, 4.5, -2.25, -23, 11.5, 20.5, -10.25, -2, 1, 0),
    (0, -18, -36, 24.5, 49, -7, -14, 0.5, 1, 0),
    (0, 18, -36, -24.5, 49, 7, -14, -0.5, 1, 0),
    (0, -3, -1, 15.75, 5.25, -15.75, -5.25, 3, 1, 0),
    (0, 3, -1, -15.75, 5.25, 15.75, -5.25, -3, 1, 0),
    (0, 9, 0, -48.25, 0, 52.5, 0, -14.25, 0, 1),
)
NEAR = (0, 1, -1, 2, -2, 0.5, -0.5, 3, -3)
SCALE = (1 / 9, 1 / 36, 1 / 36, -1 / 450, -1 / 450, -128 / 1575, -128 / 1575, 1 / 6300, 1 / 6300, 1)


def stem(image, left, right, above, below, w_patch, dw_kernel, spread, taps, ordered, pixels, split):
    rows = spread.shape[0]
    local = (rows - 6) * 4
    places = rows * 16

    def pick_rows(count, first, wanted_of):
        place, source = iota((places, count), 0), iota((places, count), 1)
        slot = place % 16
        pixel_row = (place // 16) * 4 + slot % 4 - first
        return ones_where((slot < 12) & wanted_of(source, slot // 4, pixel_row))

    pick = pick_rows(
        3 * local, 12, lambda s, c, r: (r >= 0) & (r < local) & (s == c * local + r)
    )
    pick_above = pick_rows(48, -4, lambda s, c, r: (r < 16) & (s == c * 16 + r))
    pick_below = pick_rows(48, 12 + local, lambda s, c, r: (r >= 0) & (s == c * 16 + r))
    width = image.shape[1]
    for source, base in ((image, 0), (left, width), (right, width + 128)):
        step = min(256, source.shape[1])
        for start in range(0, source.shape[1], step):
            lanes = slice(base + start, base + start + step)
            ordered[:, lanes] = (
                matmul(pick, source[:, start : start + step])
                + matmul(pick_above, above[:, lanes])
                + matmul(pick_below, below[:, lanes])
            ).astype(BF16)
    for tile in range(pixels.shape[2] // 128):
        low = max(0, 512 * tile - 32) // 128 * 128
        high = min(width, 512 * tile + 512)
        parts = [(low, high, low)]
        if 512 * tile < 32:
            parts.append((width, width + 128, -128))
        if 512 * tile + 480 > width:
            parts.append((width + 128, width + 256, width))
        found = None
        for begin, end, first in parts:
            lane, source = iota((end - begin, 512), 1), iota((end - begin, 512), 0)
            wanted = 4 * (tile * 128 + lane % 128 - 8) + lane // 128
            part = matmul(ordered[:, begin:end], ones_where(source + first == wanted))
            found = part if found is None else found + part
        found = found.astype(BF16)
        for phase in range(4):
            pixels[phase, :, tile * 128 : tile * 128 + 128] = found[:, phase * 128 : phase * 128 + 128]
    place, source = iota((64, 48), 0), iota((64, 48), 1)
    slot = place % 16
    pick = ones_where((slot < 12) & (source == slot * 4 + place // 16))
    weights = matmul(pick, w_patch[...]).astype(BF16)
    offset = iota((32, 144), 1) - 5 - 4 * iota((32, 144), 0)
    for point in range(10):
        value = jnp.zeros((32, 144), F32)
        for m in range(10):
            if SPREAD[point][m]:
                value = jnp.where(offset == m, float(SPREAD[point][m]), value)
        split[point * 32 : point * 32 + 32] = value.astype(BF16)
    for place in range(4):
        split[320 + place * 32 : 352 + place * 32] = ones_where(offset == 3 + place)
    place, source = iota((16, 7), 0), iota((16, 7), 1)
    powers = jnp.zeros((16, 7), F32)
    for point in range(10):
        for j in range(7):
            weight = float(NEAR[point] ** j) if point < 9 else float(j == 6)
            if weight:
                powers = jnp.where((place == point) & (source == j), weight, powers)
    high = powers.astype(BF16)
    low = (powers - high.astype(F32)).astype(BF16)
    for i in range(7):
        value = matmul(high, dw_kernel[i]) + matmul(low, dw_kernel[i])
        for point in range(10):
            taps[point, i] = jnp.broadcast_to(value[point : point + 1] * SCALE[point], taps.shape[2:])

    def step(row, carry):
        patches = jnp.concatenate(
            [pixels[phase, pl.ds(pl.multiple_of(row * 16, 16), 16), :] for phase in range(4)], axis=0
        )
        value = matmul(patches, weights, ((0,), (0,))).astype(BF16)
        for half in range(2):
            found = matmul(split[...], value[half * 128 : half * 128 + 144])
            spread[row, half] = found.reshape(spread.shape[2:])
        return carry

    lax.fori_loop(0, rows, step, 0, unroll=STEM)


def conv_tile(spread, taps, mixed, row, rows, blocks):
    chunks = 4 // blocks

    def step(index, carry):
        half = index // chunks
        block = pl.ds((index % chunks) * blocks, blocks)
        for start in range(0, spread.shape[5], 128):
            lanes = slice(start, start + 128)

            def products(point):
                sums = [None] * rows
                weights = [taps[point, i, :, lanes] for i in range(7)]
                for line in range(rows + 6):
                    value = spread[row + line, half, point, block, :, lanes]
                    for r in range(rows):
                        if 0 <= line - r < 7:
                            term = value * weights[line - r]
                            sums[r] = term if sums[r] is None else sums[r] + term
                return sums

            first, last = products(0), products(9)
            second, third = [0.0] * rows, [0.0] * rows
            for point in (1, 3, 5, 7):
                plus, minus = products(point), products(point + 1)
                factor = float(NEAR[point])
                for r in range(rows):
                    both, gap = plus[r] + minus[r], plus[r] - minus[r]
                    first[r] = first[r] + both
                    if point == 1:
                        second[r], third[r], last[r] = gap, both, last[r] + gap
                    else:
                        second[r] = second[r] + gap * factor
                        third[r] = third[r] + both * factor**2
                        last[r] = last[r] + gap * factor**3
            for place, found in enumerate((first, second, third, last)):
                for r in range(rows):
                    mixed[r, half, place, block, :, lanes] = found[r]
        return carry

    lax.fori_loop(0, 2 * chunks, step, 0)


def gelu_half(half):
    c = 2.0 * 0.7978845608028654
    inner = half * (c + (c * 4.0 * 0.044715) * (half * half))
    return half + half * jnp.tanh(inner)


def encoder(
    image, left, right, above, below, w_patch, dw_kernel, gain_one, scale, gain_two, query,
    w_up_far, w_down_far, w_kv_far,
    out, spread, taps, ordered, pixels, split, mixed, features, sums, w_up, w_down, w_kv, arrived,
):
    width = spread.shape[5]
    tokens = features.shape[0]
    copies = [
        pltpu.make_async_copy(far, near, arrived.at[k])
        for k, (far, near) in enumerate(((w_up_far, w_up), (w_down_far, w_down), (w_kv_far, w_kv)))
    ]
    for copy in copies:
        copy.start()
    stem(
        image, left, right, above, below, w_patch, dw_kernel, spread, taps, ordered, pixels, split
    )
    for copy in copies:
        copy.wait()
    w_up[...] = w_up[...] * jnp.asarray(0.5, BF16)
    per_tile = mixed.shape[0]
    tiles = tokens // TOKENS

    def block_step(tile, carry):
        row = tile * per_tile
        conv_tile(spread, taps, mixed, row, CONV_ROWS, CONV_BLOCKS)
        normed = layer_norm(mixed[...].reshape(TOKENS, width), gain_one[...]).astype(BF16)
        down = None
        for start in range(0, w_up.shape[1], 256):
            hidden = gelu_half(matmul(normed, w_up[:, start : start + 256])).astype(BF16)
            part = matmul(hidden, w_down[start : start + 256, :])
            down = part if down is None else down + part
        center = spread[pl.ds(row + 3, per_tile), :, 10:14].reshape(TOKENS, width)
        block = center + scale[...] * down
        features[pl.ds(pl.multiple_of(tile * TOKENS, TOKENS), TOKENS), :] = layer_norm(
            block, gain_two[...]
        ).astype(BF16)
        return carry

    lax.fori_loop(0, tiles, block_step, 0)
    pair = 2 * HEAD_DIM
    sums[...] = jnp.zeros_like(sums)
    latents = out.shape[2]
    lowest = jnp.full((1, 2 * latents), -jnp.inf, F32)
    start_stats = tuple((lowest, jnp.zeros((1, 2 * latents), F32)) for _ in range(HEADS // 2))

    def attend_step(tile, stats):
        feature = features[pl.ds(pl.multiple_of(tile * ATTEND, ATTEND), ATTEND), :]
        turned = feature.T
        result = []

        def score(p):
            keys = matmul(feature, w_kv[:, p * pair : p * pair + pair]).astype(BF16)
            return matmul(keys, query[p])

        ahead = score(0)
        for p in range(HEADS // 2):
            top, total = stats[p]
            scores = ahead
            if p + 1 < HEADS // 2:
                ahead = score(p + 1)
            top_new = jnp.maximum(top, jnp.max(scores, axis=0, keepdims=True))
            expo = jnp.exp(scores - top_new)
            factor = jnp.exp(top - top_new)
            total = total * factor + jnp.sum(expo, axis=0, keepdims=True)
            lanes = slice(p * 2 * latents, (p + 1) * 2 * latents)
            sums[:, lanes] = sums[:, lanes] * factor + matmul(turned, expo.astype(BF16))
            result.append((top_new, total))
        return tuple(result)

    stats = lax.fori_loop(0, tokens // ATTEND, attend_step, start_stats)
    per_head = out.shape[0] // HEADS
    depth = HEAD_DIM // per_head
    for head in range(HEADS):
        lanes = slice(head * latents, (head + 1) * latents)
        mine = slice((head % 2) * latents, (head % 2 + 1) * latents)
        total_sums = sums[:, lanes]
        high = total_sums.astype(BF16)
        low = (total_sums - high.astype(F32)).astype(BF16)
        first = HEADS * HEAD_DIM + head * HEAD_DIM
        weights = w_kv[:, first : first + HEAD_DIM]
        value = matmul(weights, high, ((0,), (0,))) + matmul(weights, low, ((0,), (0,)))
        lines = []
        for stat in stats[head // 2]:
            rest = stat[:, mine]
            for _ in range(3):
                piece = rest.astype(BF16).astype(F32)
                lines.append(piece)
                rest = rest - piece
        line = iota((16, latents), 0)
        extra = jnp.zeros((16, latents), F32)
        for k, piece in enumerate(lines):
            extra = jnp.where(line == k, piece, extra)
        for part in range(per_head):
            place = head * per_head + part
            out[place, :depth] = value[part * depth : (part + 1) * depth].astype(BF16)
            out[place, depth:] = extra.astype(BF16)


def split_three(value):
    high = lax.reduce_precision(value, 8, 7)
    rest = value - high
    middle = lax.reduce_precision(rest, 8, 7)
    return high, middle, rest - middle


def pack_partial(sums, top, total):
    rows = jnp.stack([*split_three(top), *split_three(total)], axis=-2)
    rows = jnp.pad(rows, ((0, 0),) * (rows.ndim - 2) + ((0, 10), (0, 0)))
    return jnp.concatenate([sums, rows], axis=-2).astype(BF16)


def merge_partials(packed):
    packed = packed.astype(F32)
    count = packed.shape[1] - 16
    stats = packed[:, count:]
    top = (stats[:, 0] + stats[:, 1]) + stats[:, 2]
    total = (stats[:, 3] + stats[:, 4]) + stats[:, 5]
    top_all = jnp.max(top, axis=0)
    factor = jnp.exp(top - top_all)
    sums = jnp.sum(packed[:, :count] * factor[:, None], axis=0)
    return sums, top_all, jnp.sum(total * factor, axis=0)


def share(value, axis):
    size = lax.axis_size(axis)
    return lax.all_to_all(jnp.broadcast_to(value, (size, *value.shape)), axis, 0, 0)


def queries(latents, gain, w_q, out):
    count = latents.shape[0]
    normed = layer_norm(latents[...].astype(F32), gain[...]).astype(BF16)
    for head in range(HEADS):
        lanes = slice(head * HEAD_DIM, (head + 1) * HEAD_DIM)
        query = (matmul(normed, w_q[:, lanes]) * HEAD_DIM ** (-0.5)).astype(BF16)
        turned = query.astype(F32).T.astype(BF16)
        empty = jnp.zeros((HEAD_DIM, count), BF16)
        rows = slice((head % 2) * HEAD_DIM, (head % 2 + 1) * HEAD_DIM)
        out[head // 2, rows, :count] = turned if head % 2 == 0 else empty
        out[head // 2, rows, count:] = empty if head % 2 == 0 else turned


def paired_queries(latents, gain_three, w_q):
    count, width = latents.shape
    return pl.pallas_call(
        queries,
        out_shape=jax.ShapeDtypeStruct((HEADS // 2, 2 * HEAD_DIM, 2 * count), BF16),
        in_specs=[pl.BlockSpec(memory_space=pltpu.VMEM)] * 3,
        out_specs=pl.BlockSpec(memory_space=pltpu.VMEM),
        cost_estimate=pl.CostEstimate(
            flops=2 * count * width * w_q.shape[1], bytes_accessed=2 * w_q.size, transcendentals=0
        ),
        name="queries",
    )(latents, gain_three.reshape(1, width), w_q)


def partial_sums(
    image, left, right, above, below, w_patch, dw_kernel, gain_one, w_up, w_down, scale_block, gain_two,
    w_kv, pairs, cols,
):
    channels, height, breadth = image.shape
    tile_rows, tile_cols = height // 4, breadth // 4
    count, width = pairs.shape[2] // 2, w_patch.shape[1]
    return pl.pallas_call(
        encoder,
        out_shape=jax.ShapeDtypeStruct((cols, HEADS * HEAD_DIM // cols + 16, count), BF16),
        in_specs=[pl.BlockSpec(memory_space=pltpu.VMEM)] * 11 + [pl.BlockSpec(memory_space=pl.ANY)] * 3,
        out_specs=pl.BlockSpec(memory_space=pltpu.VMEM),
        scratch_shapes=[
            pltpu.VMEM((tile_rows + 6, 2, 14, 4, 8, width), F32),
            pltpu.VMEM((10, 7, 8, width), F32),
            pltpu.VMEM(((tile_rows + 6) * 16, breadth + 256), BF16),
            pltpu.VMEM((4, (tile_rows + 6) * 16, tile_cols + 128), BF16),
            pltpu.VMEM((448, 144), BF16),
            pltpu.VMEM((TOKENS // tile_cols, 2, 4, 4, 8, width), F32),
            pltpu.VMEM((tile_rows * tile_cols, width), BF16),
            pltpu.VMEM((width, HEADS * count), F32),
            pltpu.VMEM(w_up.shape, BF16),
            pltpu.VMEM(w_down.shape, BF16),
            pltpu.VMEM(w_kv.shape, BF16),
            pltpu.SemaphoreType.DMA((3,)),
        ],
        compiler_params=pltpu.CompilerParams(vmem_limit_bytes=52 * 2**20),
        name="encoder",
    )(
        image.reshape(channels * height, breadth),
        left.reshape(channels * height, 128),
        right.reshape(channels * height, 128),
        above.reshape(channels * 16, breadth + 256),
        below.reshape(channels * 16, breadth + 256),
        w_patch,
        dw_kernel,
        gain_one.reshape(1, width),
        scale_block.reshape(1, width),
        gain_two.reshape(1, width),
        pairs,
        w_up,
        w_down,
        w_kv,
    )


def project(attended, w_o, latents, out):
    out[...] = latents[...].astype(F32) + matmul(attended[...], w_o[...], ((0,), (0,)))


def body(
    image,
    w_patch,
    dw_kernel,
    gain_one,
    w_up,
    w_down,
    scale_block,
    gain_two,
    w_kv,
    latents,
    gain_three,
    w_q,
    w_o,
):
    cols = lax.axis_size("cols")
    left, right = exchange(image[:, :, -128:], image[:, :, :128], "cols")
    above, below = exchange(
        *(
            jnp.concatenate([image[:, rows], left[:, rows], right[:, rows]], axis=2)
            for rows in (slice(-16, None), slice(0, 16))
        ),
        "rows",
    )
    pairs = paired_queries(latents, gain_three, w_q)
    packed = partial_sums(
        image, left, right, above, below, w_patch, dw_kernel, gain_one, w_up, w_down, scale_block,
        gain_two, w_kv, pairs, cols,
    )
    partial = merge_partials(lax.all_to_all(packed, "cols", 0, 0))
    sums, _, total = merge_partials(share(pack_partial(*partial), "rows"))
    attended = share((sums / total).astype(BF16), "cols").reshape(HEADS * HEAD_DIM, -1)
    return pl.pallas_call(
        project,
        out_shape=jax.ShapeDtypeStruct(latents.shape, F32),
        in_specs=[pl.BlockSpec(memory_space=pltpu.VMEM)] * 3,
        out_specs=pl.BlockSpec(memory_space=pltpu.VMEM),
        name="project",
    )(attended, w_o, latents)


def solution(mesh):
    in_specs = (P(None, "rows", "cols"), P(), P(), P(), P(), P(), P(), P(), P(), P(), P(), P(), P())
    out_specs = P()
    return jax.shard_map(body, mesh=mesh, in_specs=in_specs, out_specs=out_specs, check_vma=False)
```

```python
import jax
import jax.numpy as jnp
import numpy as np
from jax import lax
from jax.experimental import pallas as pl
from jax.experimental.pallas import tpu as pltpu
from jax.sharding import PartitionSpec as P

HEADS = 8
HEAD_DIM = 128
F32 = jnp.float32
BF16 = jnp.bfloat16
TOKENS = 1024
ATTEND = 4096
CONV_ROWS = 4
CONV_BLOCKS = 1


def exchange(last, first, axis):
    devices = lax.axis_size(axis)
    up = [(i, i + 1) for i in range(devices - 1)]
    down = [(j, i) for i, j in up]
    return lax.ppermute(last, axis, up), lax.ppermute(first, axis, down)


def layer_norm(values, gain):
    center = values - jnp.mean(values, axis=-1, keepdims=True)
    spread = jnp.mean(center * center, axis=-1, keepdims=True)
    return center * lax.rsqrt(spread + 1e-06) * gain


def matmul(left, right, dims=((1,), (0,))):
    return lax.dot_general(left, right, (dims, ((), ())), preferred_element_type=F32)


def iota(shape, dim):
    return lax.broadcasted_iota(jnp.int32, shape, dim)


def ones_where(mask):
    return jnp.where(mask, 1.0, 0.0).astype(BF16)


SPREAD = (
    (9, 0, -48.25, 0, 52.5, 0, -14.25, 0, 1, 0),
    (0, -9, -9, 39.25, 39.25, -13.25, -13.25, 1, 1, 0),
    (0, 9, -9, -39.25, 39.25, 13.25, -13.25, -1, 1, 0),
    (0, -4.5, -2.25, 23, 11.5, -20.5, -10.25, 2, 1, 0),
    (0, 4.5, -2.25, -23, 11.5, 20.5, -10.25, -2, 1, 0),
    (0, -18, -36, 24.5, 49, -7, -14, 0.5, 1, 0),
    (0, 18, -36, -24.5, 49, 7, -14, -0.5, 1, 0),
    (0, -3, -1, 15.75, 5.25, -15.75, -5.25, 3, 1, 0),
    (0, 3, -1, -15.75, 5.25, 15.75, -5.25, -3, 1, 0),
    (0, 9, 0, -48.25, 0, 52.5, 0, -14.25, 0, 1),
)
NEAR = (0, 1, -1, 2, -2, 0.5, -0.5, 3, -3)
SCALE = (1 / 9, 1 / 36, 1 / 36, -1 / 450, -1 / 450, -128 / 1575, -128 / 1575, 1 / 6300, 1 / 6300, 1)


def tile_parts(width, tiles):
    result = []
    for tile in range(tiles):
        low = max(0, 512 * tile - 32) // 128 * 128
        parts = [(low, min(width, 512 * tile + 512), low)]
        if 512 * tile < 32:
            parts.append((width, width + 128, -128))
        if 512 * tile + 480 > width:
            parts.append((width + 128, width + 256, width))
        result.append(parts)
    return result


def tables(rows, width, tiles):
    local = (rows - 6) * 4
    place = np.arange(rows * 16)[:, None]
    slot = place % 16
    pixel_row = place // 16 * 4 + slot % 4
    result = []
    spans = ((local, 12, 48, -48), (16, -4, 0, 48), (16, 12 + local, -48, None))
    for height, first, begin, end in spans:
        line = pixel_row - first
        inside = (slot < 12) & (line >= 0) & (line < height)
        table = inside & (np.arange(3 * height) == slot // 4 * height + line)
        result.append(table[begin:end])
    lane = np.arange(512)
    for tile, parts in enumerate(tile_parts(width, tiles)):
        wanted = 4 * (tile * 128 + lane % 128 - 8) + lane // 128
        result += [np.arange(end - begin)[:, None] + first == wanted for begin, end, first in parts]
    offset = np.arange(144) - 5 - 4 * np.arange(32)[:, None]
    spread = [sum(value * (offset == m) for m, value in enumerate(line)) for line in SPREAD]
    result.append(np.concatenate(spread + [1.0 * (offset == 3 + place) for place in range(4)]))
    return [jnp.asarray(table.astype(np.float32), BF16) for table in result]


def stem(image, left, right, above, below, w_patch, dw_kernel, chosen, taps, ordered, pixels):
    pick, pick_above, pick_below, *splits = chosen
    width = image.shape[1]
    below_row = ordered.shape[0] - 48
    for source, base in ((image, 0), (left, width), (right, width + 128)):
        step = min(256, source.shape[1])
        for start in range(0, source.shape[1], step):
            lanes = slice(base + start, base + start + step)
            ordered[48:below_row, lanes] = matmul(
                pick[...], source[:, start : start + step]
            ).astype(BF16)
            ordered[:48, lanes] = matmul(pick_above[...], above[:, lanes]).astype(BF16)
            ordered[below_row:, lanes] = matmul(pick_below[...], below[:, lanes]).astype(BF16)
    for tile, parts in enumerate(tile_parts(width, pixels.shape[2] // 128)):
        found = None
        for begin, end, _ in parts:
            part = matmul(ordered[:, begin:end], splits.pop(0)[...])
            found = part if found is None else found + part
        found = found.astype(BF16)
        for phase in range(4):
            pixels[phase, :, tile * 128 : tile * 128 + 128] = found[:, phase * 128 : phase * 128 + 128]
    place, source = iota((64, 48), 0), iota((64, 48), 1)
    slot = place % 16
    pick = ones_where((slot < 12) & (source == slot * 4 + place // 16))
    weights = matmul(pick, w_patch[...]).astype(BF16)
    place, source = iota((16, 7), 0), iota((16, 7), 1)
    powers = jnp.zeros((16, 7), F32)
    for point in range(10):
        for j in range(7):
            weight = float(NEAR[point] ** j) if point < 9 else float(j == 6)
            if weight:
                powers = jnp.where((place == point) & (source == j), weight, powers)
    high = powers.astype(BF16)
    low = (powers - high.astype(F32)).astype(BF16)
    for i in range(7):
        value = matmul(high, dw_kernel[i]) + matmul(low, dw_kernel[i])
        for point in range(10):
            taps[point, i] = jnp.broadcast_to(value[point : point + 1] * SCALE[point], taps.shape[2:])

    return weights


def stem_row(row, weights, split, spread, pixels):
    patches = jnp.concatenate(
        [pixels[phase, row * 16 : row * 16 + 16, :] for phase in range(4)], axis=0
    )
    value = matmul(patches, weights, ((0,), (0,))).astype(BF16)
    for half in range(2):
        found = matmul(split[...], value[half * 128 : half * 128 + 144])
        spread[row, half] = found.reshape(spread.shape[2:])


def conv_tile(spread, taps, mixed, row, rows, blocks):
    chunks = 4 // blocks

    def step(index, carry):
        half = index // chunks
        block = pl.ds((index % chunks) * blocks, blocks)
        for start in range(0, spread.shape[5], 128):
            lanes = slice(start, start + 128)

            def products(point):
                sums = [None] * rows
                weights = [taps[point, i, :, lanes] for i in range(7)]
                for line in range(rows + 6):
                    value = spread[row + line, half, point, block, :, lanes]
                    for r in range(rows):
                        if 0 <= line - r < 7:
                            term = value * weights[line - r]
                            sums[r] = term if sums[r] is None else sums[r] + term
                return sums

            first, last = products(0), products(9)
            second, third = [0.0] * rows, [0.0] * rows
            for point in (1, 3, 5, 7):
                plus, minus = products(point), products(point + 1)
                factor = float(NEAR[point])
                for r in range(rows):
                    both, gap = plus[r] + minus[r], plus[r] - minus[r]
                    first[r] = first[r] + both
                    if point == 1:
                        second[r], third[r], last[r] = gap, both, last[r] + gap
                    else:
                        second[r] = second[r] + gap * factor
                        third[r] = third[r] + both * factor**2
                        last[r] = last[r] + gap * factor**3
            for place, found in enumerate((first, second, third, last)):
                for r in range(rows):
                    mixed[r, half, place, block, :, lanes] = found[r]
        return carry

    lax.fori_loop(0, 2 * chunks, step, 0)


def gelu_half(half):
    c = 2.0 * 0.7978845608028654
    inner = half * (c + (c * 4.0 * 0.044715) * (half * half))
    return half + half * jnp.tanh(inner)


def encoder(
    image, left, right, above, below, w_patch, dw_kernel, gain_one, scale, gain_two,
    w_up_far, w_down_far, w_kv_far, query_far, *rest,
):
    *chosen, split = rest[:-13]
    (
        out, spread, taps, ordered, pixels, mixed, features, sums, w_up, w_down, w_kv, query, arrived,
    ) = rest[-13:]
    width = spread.shape[5]
    tokens = features.shape[0]
    copies = [
        pltpu.make_async_copy(far, near, arrived.at[k])
        for k, (far, near) in enumerate(
            ((w_up_far, w_up), (w_down_far, w_down), (w_kv_far, w_kv), (query_far, query))
        )
    ]
    for copy in copies:
        copy.start()
    weights = stem(
        image, left, right, above, below, w_patch, dw_kernel, chosen, taps, ordered, pixels
    )
    rows, per_tile = spread.shape[0], mixed.shape[0]
    for row in range(per_tile + 6):
        stem_row(row, weights, split, spread, pixels)
    for copy in copies:
        copy.wait()
    w_up[...] = w_up[...] * jnp.asarray(0.5, BF16)
    for tile in range(tokens // TOKENS):
        row = tile * per_tile
        conv_tile(spread, taps, mixed, row, CONV_ROWS, CONV_BLOCKS)
        center = spread[row + 3 : row + 3 + per_tile, :, 10:14].reshape(TOKENS, width)
        ahead = list(range(row + per_tile + 6, min(rows, row + 2 * per_tile + 6)))
        normed = layer_norm(mixed[...].reshape(TOKENS, width), gain_one[...]).astype(BF16)
        down = None
        for start in range(0, w_up.shape[1], 256):
            hidden = gelu_half(matmul(normed, w_up[:, start : start + 256])).astype(BF16)
            part = matmul(hidden, w_down[start : start + 256, :])
            down = part if down is None else down + part
            if ahead:
                stem_row(ahead.pop(0), weights, split, spread, pixels)
        block = center + scale[...] * down
        features[tile * TOKENS : (tile + 1) * TOKENS, :] = layer_norm(block, gain_two[...]).astype(
            BF16
        )
    pair = 2 * HEAD_DIM
    sums[...] = jnp.zeros_like(sums)
    latents = out.shape[2]
    lowest = jnp.full((1, 2 * latents), -jnp.inf, F32)
    start_stats = tuple((lowest, jnp.zeros((1, 2 * latents), F32)) for _ in range(HEADS // 2))

    def attend_step(tile, stats):
        feature = features[pl.ds(pl.multiple_of(tile * ATTEND, ATTEND), ATTEND), :]
        turned = feature.T
        result = []

        def score(p):
            keys = matmul(feature, w_kv[:, p * pair : p * pair + pair]).astype(BF16)
            return matmul(keys, query[p])

        ahead = score(0)
        for p in range(HEADS // 2):
            top, total = stats[p]
            scores = ahead
            if p + 1 < HEADS // 2:
                ahead = score(p + 1)
            top_new = jnp.maximum(top, jnp.max(scores, axis=0, keepdims=True))
            expo = jnp.exp(scores - top_new)
            factor = jnp.exp(top - top_new)
            total = total * factor + jnp.sum(expo, axis=0, keepdims=True)
            lanes = slice(p * 2 * latents, (p + 1) * 2 * latents)
            sums[:, lanes] = sums[:, lanes] * factor + matmul(turned, expo.astype(BF16))
            result.append((top_new, total))
        return tuple(result)

    stats = lax.fori_loop(0, tokens // ATTEND, attend_step, start_stats)
    per_head = out.shape[0] // HEADS
    depth = HEAD_DIM // per_head
    for head in range(HEADS):
        lanes = slice(head * latents, (head + 1) * latents)
        mine = slice((head % 2) * latents, (head % 2 + 1) * latents)
        total_sums = sums[:, lanes]
        high = total_sums.astype(BF16)
        low = (total_sums - high.astype(F32)).astype(BF16)
        first = HEADS * HEAD_DIM + head * HEAD_DIM
        weights = w_kv[:, first : first + HEAD_DIM]
        value = matmul(weights, high, ((0,), (0,))) + matmul(weights, low, ((0,), (0,)))
        lines = []
        for stat in stats[head // 2]:
            rest = stat[:, mine]
            for _ in range(3):
                piece = rest.astype(BF16).astype(F32)
                lines.append(piece)
                rest = rest - piece
        line = iota((16, latents), 0)
        extra = jnp.zeros((16, latents), F32)
        for k, piece in enumerate(lines):
            extra = jnp.where(line == k, piece, extra)
        for part in range(per_head):
            place = head * per_head + part
            out[place, :depth] = value[part * depth : (part + 1) * depth].astype(BF16)
            out[place, depth:] = extra.astype(BF16)


def split_three(value):
    high = lax.reduce_precision(value, 8, 7)
    rest = value - high
    middle = lax.reduce_precision(rest, 8, 7)
    return high, middle, rest - middle


def pack_partial(sums, top, total):
    rows = jnp.stack([*split_three(top), *split_three(total)], axis=-2)
    rows = jnp.pad(rows, ((0, 0),) * (rows.ndim - 2) + ((0, 10), (0, 0)))
    return jnp.concatenate([sums, rows], axis=-2).astype(BF16)


def merge_partials(packed):
    packed = packed.astype(F32)
    count = packed.shape[1] - 16
    stats = packed[:, count:]
    top = (stats[:, 0] + stats[:, 1]) + stats[:, 2]
    total = (stats[:, 3] + stats[:, 4]) + stats[:, 5]
    top_all = jnp.max(top, axis=0)
    factor = jnp.exp(top - top_all)
    sums = jnp.sum(packed[:, :count] * factor[:, None], axis=0)
    return sums, top_all, jnp.sum(total * factor, axis=0)


def share(value, axis):
    size = lax.axis_size(axis)
    return lax.all_to_all(jnp.broadcast_to(value, (size, *value.shape)), axis, 0, 0)


def queries(latents, gain, w_q, out):
    count = latents.shape[0]
    normed = layer_norm(latents[...].astype(F32), gain[...]).astype(BF16)
    for head in range(HEADS):
        lanes = slice(head * HEAD_DIM, (head + 1) * HEAD_DIM)
        query = (matmul(normed, w_q[:, lanes]) * HEAD_DIM ** (-0.5)).astype(BF16)
        turned = query.astype(F32).T.astype(BF16)
        empty = jnp.zeros((HEAD_DIM, count), BF16)
        rows = slice((head % 2) * HEAD_DIM, (head % 2 + 1) * HEAD_DIM)
        out[head // 2, rows, :count] = turned if head % 2 == 0 else empty
        out[head // 2, rows, count:] = empty if head % 2 == 0 else turned


def paired_queries(latents, gain_three, w_q):
    count, width = latents.shape
    return pl.pallas_call(
        queries,
        out_shape=jax.ShapeDtypeStruct((HEADS // 2, 2 * HEAD_DIM, 2 * count), BF16),
        in_specs=[pl.BlockSpec(memory_space=pltpu.VMEM)] * 3,
        out_specs=pl.BlockSpec(memory_space=pltpu.VMEM),
        cost_estimate=pl.CostEstimate(
            flops=2 * count * width * w_q.shape[1], bytes_accessed=2 * w_q.size, transcendentals=0
        ),
        name="queries",
    )(latents, gain_three.reshape(1, width), w_q)


def partial_sums(
    image, left, right, above, below, w_patch, dw_kernel, gain_one, w_up, w_down, scale_block, gain_two,
    w_kv, pairs, cols,
):
    channels, height, breadth = image.shape
    tile_rows, tile_cols = height // 4, breadth // 4
    count, width = pairs.shape[2] // 2, w_patch.shape[1]
    fixed = tables(tile_rows + 6, breadth, tile_cols // 128 + 1)
    return pl.pallas_call(
        encoder,
        out_shape=jax.ShapeDtypeStruct((cols, HEADS * HEAD_DIM // cols + 16, count), BF16),
        in_specs=[pl.BlockSpec(memory_space=pltpu.VMEM)] * 10 + [pl.BlockSpec(memory_space=pl.ANY)] * 4
        + [pl.BlockSpec(memory_space=pltpu.VMEM)] * len(fixed),
        out_specs=pl.BlockSpec(memory_space=pltpu.VMEM),
        scratch_shapes=[
            pltpu.VMEM((tile_rows + 6, 2, 14, 4, 8, width), F32),
            pltpu.VMEM((10, 7, 8, width), F32),
            pltpu.VMEM(((tile_rows + 6) * 16, breadth + 256), BF16),
            pltpu.VMEM((4, (tile_rows + 6) * 16, tile_cols + 128), BF16),
            pltpu.VMEM((TOKENS // tile_cols, 2, 4, 4, 8, width), F32),
            pltpu.VMEM((tile_rows * tile_cols, width), BF16),
            pltpu.VMEM((width, HEADS * count), F32),
            pltpu.VMEM(w_up.shape, BF16),
            pltpu.VMEM(w_down.shape, BF16),
            pltpu.VMEM(w_kv.shape, BF16),
            pltpu.VMEM(pairs.shape, BF16),
            pltpu.SemaphoreType.DMA((4,)),
        ],
        compiler_params=pltpu.CompilerParams(vmem_limit_bytes=52 * 2**20),
        name="encoder",
    )(
        image.reshape(channels * height, breadth),
        left.reshape(channels * height, 128),
        right.reshape(channels * height, 128),
        above.reshape(channels * 16, breadth + 256),
        below.reshape(channels * 16, breadth + 256),
        w_patch,
        dw_kernel,
        gain_one.reshape(1, width),
        scale_block.reshape(1, width),
        gain_two.reshape(1, width),
        w_up,
        w_down,
        w_kv,
        pairs,
        *fixed,
    )


def project(attended, w_o, latents, out):
    out[...] = latents[...].astype(F32) + matmul(attended[...], w_o[...], ((0,), (0,)))


def body(
    image,
    w_patch,
    dw_kernel,
    gain_one,
    w_up,
    w_down,
    scale_block,
    gain_two,
    w_kv,
    latents,
    gain_three,
    w_q,
    w_o,
):
    cols = lax.axis_size("cols")
    left, right = exchange(image[:, :, -128:], image[:, :, :128], "cols")
    above, below = exchange(
        *(
            jnp.concatenate([image[:, rows], left[:, rows], right[:, rows]], axis=2)
            for rows in (slice(-16, None), slice(0, 16))
        ),
        "rows",
    )
    pairs = paired_queries(latents, gain_three, w_q)
    packed = partial_sums(
        image, left, right, above, below, w_patch, dw_kernel, gain_one, w_up, w_down, scale_block,
        gain_two, w_kv, pairs, cols,
    )
    partial = merge_partials(lax.all_to_all(packed, "cols", 0, 0))
    sums, _, total = merge_partials(share(pack_partial(*partial), "rows"))
    attended = share((sums / total).astype(BF16), "cols").reshape(HEADS * HEAD_DIM, -1)
    return pl.pallas_call(
        project,
        out_shape=jax.ShapeDtypeStruct(latents.shape, F32),
        in_specs=[pl.BlockSpec(memory_space=pltpu.VMEM)] * 3,
        out_specs=pl.BlockSpec(memory_space=pltpu.VMEM),
        name="project",
    )(attended, w_o, latents)


def solution(mesh):
    in_specs = (P(None, "rows", "cols"), P(), P(), P(), P(), P(), P(), P(), P(), P(), P(), P(), P())
    out_specs = P()
    return jax.shard_map(body, mesh=mesh, in_specs=in_specs, out_specs=out_specs, check_vma=False)
```
